32 devices in a mesh: seq: 8 (over z, y), ch: 4 (over x, core).
Axes of the slice: x: 2, y: 2, z: 4, core: 2. Of those that a mesh axis runs over, the one named last changes fastest.
Arguments:
- query_rows: bfloat16 [2048, 4096], P(('seq', 'ch')), may hold values from -6 to 6
- key_rows: bfloat16 [2048, 4096], P(('seq', 'ch')), may hold values from -6 to 6
- value_rows: bfloat16 [2048, 4096], P(('seq', 'ch')), may hold values from -6 to 6
- filter_taps: float32 [2048, 4096], P(('seq', 'ch')), may hold values from -1.1 to 1.1
- skip_gain: float32 [4096], replicated, may hold values from 0.5 to 1.5
Outputs:
- gated_output: bfloat16 [2048, 4096], P(('seq', 'ch'))
The draws below stay inside these ranges and needn't reach their ends.
All inputs are finite; a program needn't handle non-finite values.
Results may differ from the reference program's by a relative error of at most 0.0014.
Values sent between devices are 32-bit elements; how exact they have to be, the bound alone decides.
A program may use at most 128 MiB of HBM per device.

```python
import math
import jax
import jax.numpy as jnp
from jax import lax

CHANNELS = 4096
SEQUENCE_TOKENS = 2048


def amplitude_for(decay_rate):
    return jnp.sqrt(2.0 * decay_rate / (1.0 - jnp.exp(-2.0 * decay_rate * SEQUENCE_TOKENS)))


def draw_filter_taps(key, part):
    random_subkeys = jax.random.split(key, 8)
    filter_draw = jax.random.truncated_normal(random_subkeys[0], -4.0, 4.0, (SEQUENCE_TOKENS, CHANNELS), jnp.float32)
    quick_share = 0.5
    quick_mask = jax.random.bernoulli(random_subkeys[1], quick_share, (CHANNELS,))
    quick_rate = jnp.exp(jax.random.uniform(random_subkeys[2], (CHANNELS,), jnp.float32, math.log(1.0 / 50.0), math.log(1.0 / 30.0)))
    slow_rate = jnp.exp(jax.random.uniform(random_subkeys[3], (CHANNELS,), jnp.float32, math.log(0.1), math.log(2.0))) / SEQUENCE_TOKENS
    tail_rate = jnp.exp(jax.random.uniform(random_subkeys[6], (CHANNELS,), jnp.float32, math.log(0.1), math.log(2.0))) / SEQUENCE_TOKENS
    tail_share = jax.random.uniform(random_subkeys[7], (CHANNELS,), jnp.float32, 0.05, 0.2)
    delay_steps = jnp.arange(SEQUENCE_TOKENS, dtype=jnp.float32)[:, None]
    quick_envelope = jnp.sqrt(1.0 - tail_share)[None, :] * amplitude_for(quick_rate)[None, :] * jnp.exp(-quick_rate[None, :] * delay_steps) + jnp.sqrt(tail_share)[None, :] * amplitude_for(tail_rate)[None, :] * jnp.exp(-tail_rate[None, :] * delay_steps)
    slow_envelope = amplitude_for(slow_rate)[None, :] * jnp.exp(-slow_rate[None, :] * delay_steps)
    decay_envelope = jnp.where(quick_mask[None, :], quick_envelope, slow_envelope)
    spike_position = jax.random.randint(random_subkeys[4], (3,), 0, SEQUENCE_TOKENS)
    falloff_amount = jax.random.uniform(random_subkeys[5], (3,), jnp.float32, 0.5, 0.8)
    for spike_index in range(3):
        decay_envelope = decay_envelope * jnp.where(delay_steps >= spike_position[spike_index].astype(jnp.float32), falloff_amount[spike_index], 1.0)
    return filter_draw * decay_envelope


def block_levels(key, dims, cuts, low, largest):
    factor_of, own = 1.0, jax.random.fold_in(key, 6)
    for dim, shards_of in cuts:
        draws = jnp.exp(jax.random.uniform(jax.random.fold_in(own, dim), (shards_of,), jnp.float32, low / len(cuts), largest / len(cuts)))
        factor_of = factor_of * jnp.repeat(draws, dims[dim] // shards_of).reshape([-1 if axis == dim else 1 for axis in range(len(dims))])
    return factor_of


def centred(stream_key, extent, scale, reach, cuts=(), kind=jnp.bfloat16):
    values = jax.random.normal(stream_key, extent, jnp.float32) * scale
    if len(cuts) > 0:
        values = block_levels(stream_key, extent, cuts, -0.22, 0.18) * values
    return jnp.clip(values, min=-reach, max=reach).astype(kind)


def setup_inputs(seed: int = 0) -> dict:
    key_of = jax.random.split(jax.random.key(seed), 6)
    query_rows = centred(key_of[0], (SEQUENCE_TOKENS, CHANNELS), 1.0, 6.0, ((0, 32),))
    key_rows = centred(key_of[1], (SEQUENCE_TOKENS, CHANNELS), 1.0, 6.0, ((0, 32),))
    value_rows = centred(key_of[2], (SEQUENCE_TOKENS, CHANNELS), 1.0, 6.0, ((0, 32),))
    filter_taps = draw_filter_taps(jax.random.fold_in(key_of[5], 71), 0)
    skip_gain = jnp.clip(jax.random.uniform(key_of[4], (CHANNELS,), jnp.float32, 0.5, 1.5), 0.5, 1.5)
    return {"query_rows": query_rows, "key_rows": key_rows, "value_rows": value_rows, "filter_taps": filter_taps, "skip_gain": skip_gain}


def convolve_block(pieces):
    signal_block, taps_block = pieces
    padded = 2 * signal_block.shape[0]
    spectrum = jnp.fft.rfft(signal_block, n=padded, axis=0) * jnp.fft.rfft(taps_block, n=padded, axis=0)
    return jnp.fft.irfft(spectrum, n=padded, axis=0)[: signal_block.shape[0]]


def reference(query_rows, key_rows, value_rows, filter_taps, skip_gain):
    signal = key_rows.astype(jnp.float32) * value_rows.astype(jnp.float32)
    block_width = min(256, CHANNELS)
    block_count = CHANNELS // block_width
    split_signal = signal.reshape(SEQUENCE_TOKENS, block_count, block_width).transpose(1, 0, 2)
    split_taps = filter_taps.reshape(SEQUENCE_TOKENS, block_count, block_width).transpose(1, 0, 2)
    convolved = lax.map(convolve_block, (split_signal, split_taps))
    convolved = convolved.transpose(1, 0, 2).reshape(SEQUENCE_TOKENS, CHANNELS).astype(jnp.float32)
    gated = query_rows.astype(jnp.float32) * (convolved + skip_gain[None, :] * signal)
    return gated.astype(jnp.bfloat16)
```

```python
import functools
import math

import jax
import jax.numpy as jnp
import ml_dtypes
import numpy as np
from jax import lax
from jax.experimental import pallas as pl
from jax.experimental.pallas import tpu as pltpu
from jax.sharding import PartitionSpec as P

highest = lax.Precision.HIGHEST


def angles(product_ids, modulus):
    return 2.0 * math.pi / modulus * (product_ids % modulus).astype(jnp.float32)


def contract(pattern, weights, operand):
    return jnp.einsum(
        pattern, weights, operand, precision=highest, preferred_element_type=jnp.float32
    )


def staged_shards(query_rows, key_rows, value_rows, filter_taps, skip_gain):
    seq_count = lax.axis_size("seq")
    group_count = lax.axis_size("ch")
    position = lax.axis_index("seq")
    row_count, full_width = key_rows.shape
    per_peer = row_count // seq_count
    columns = full_width // group_count
    local_rows = group_count * per_peer
    tokens = row_count * group_count
    slot_count = 2 * seq_count
    length = 2 * tokens * seq_count
    signal = key_rows.astype(jnp.float32) * value_rows.astype(jnp.float32)
    layout = (1, seq_count, 1, per_peer, full_width)
    moved_signal, moved_filter = (
        lax.all_to_all(
            lax.all_to_all(signal.reshape(layout), "seq", split_axis=1, concat_axis=0, tiled=True),
            "ch",
            split_axis=4,
            concat_axis=2,
            tiled=True,
        ),
        lax.all_to_all(
            lax.all_to_all(
                filter_taps.reshape(layout), "seq", split_axis=1, concat_axis=0, tiled=True
            ),
            "ch",
            split_axis=4,
            concat_axis=2,
            tiled=True,
        ),
    )
    moved_signal = moved_signal.reshape(seq_count, local_rows, columns)
    moved_filter = moved_filter.reshape(seq_count, local_rows, columns)
    slot_ids = jnp.arange(slot_count, dtype=jnp.int32)
    owners = slot_ids // 2
    freq_slot = jnp.where(
        slot_ids % 2 == 0, owners, jnp.where(owners == 0, seq_count, slot_count - owners)
    )
    blocks = jnp.arange(seq_count, dtype=jnp.int32)
    block_phase = angles(freq_slot[:, None] * blocks[None, :], slot_count)
    block_cos = jnp.cos(block_phase)
    block_sin = jnp.sin(block_phase)
    local_ids = jnp.arange(local_rows, dtype=jnp.int32)
    local_time = local_ids // per_peer * row_count + position * per_peer + local_ids % per_peer
    twist_angle = -angles(freq_slot[:, None] * local_time[None, :], length)
    twist_cos = jnp.cos(twist_angle)[:, :, None]
    twist_sin = jnp.sin(twist_angle)[:, :, None]

    def forward_blocks(real_part):
        out_real = contract("jd,dmc->jmc", block_cos, real_part)
        out_imag = -contract("jd,dmc->jmc", block_sin, real_part)
        return jnp.stack(
            [
                out_real * twist_cos - out_imag * twist_sin,
                out_real * twist_sin + out_imag * twist_cos,
            ]
        )

    all_ids = jnp.arange(tokens, dtype=jnp.int32)
    peer_id = all_ids // local_rows
    within = all_ids % local_rows
    all_time = within // per_peer * row_count + peer_id * per_peer + within % per_peer
    inner_phase = angles(all_ids[:, None] * all_time[None, :], tokens)
    inner_cos = jnp.cos(inner_phase)
    inner_sin = jnp.sin(inner_phase)

    def forward_inner(spectrum):
        real_part = spectrum[0]
        imag_part = spectrum[1]
        out_real = contract("qp,jpc->jqc", inner_cos, real_part) + contract(
            "qp,jpc->jqc", inner_sin, imag_part
        )
        out_imag = contract("qp,jpc->jqc", inner_cos, imag_part) - contract(
            "qp,jpc->jqc", inner_sin, real_part
        )
        return (out_real, out_imag)

    signal_spectrum, filter_spectrum = (
        lax.all_to_all(
            forward_blocks(moved_signal), "seq", split_axis=1, concat_axis=2, tiled=True
        ),
        lax.all_to_all(
            forward_blocks(moved_filter), "seq", split_axis=1, concat_axis=2, tiled=True
        ),
    )
    signal_real, signal_imag = forward_inner(signal_spectrum)
    filter_real, filter_imag = forward_inner(filter_spectrum)
    product_real = signal_real * filter_real - signal_imag * filter_imag
    product_imag = signal_real * filter_imag + signal_imag * filter_real
    back_real = contract("qp,jqc->jpc", inner_cos, product_real) - contract(
        "qp,jqc->jpc", inner_sin, product_imag
    )
    back_imag = contract("qp,jqc->jpc", inner_cos, product_imag) + contract(
        "qp,jqc->jpc", inner_sin, product_real
    )
    my_slots = jnp.stack([position, jnp.where(position == 0, seq_count, slot_count - position)])
    back_phase = angles(my_slots[:, None] * all_time[None, :], length)[:, :, None]
    back_cos = jnp.cos(back_phase)
    back_sin = jnp.sin(back_phase)
    turned_real = back_real * back_cos - back_imag * back_sin
    turned_imag = back_real * back_sin + back_imag * back_cos
    inverse_scale = 1.0 / length
    gathered = lax.all_to_all(
        jnp.stack([turned_real, turned_imag]), "seq", split_axis=2, concat_axis=1, tiled=True
    )
    convolved = (
        contract("jd,jmc->dmc", block_cos, gathered[0])
        - contract("jd,jmc->dmc", block_sin, gathered[1])
    ) * inverse_scale
    returned = lax.all_to_all(
        lax.all_to_all(
            convolved.reshape(seq_count, 1, group_count, per_peer, columns),
            "seq",
            split_axis=0,
            concat_axis=1,
            tiled=True,
        ),
        "ch",
        split_axis=2,
        concat_axis=4,
        tiled=True,
    )
    convolved_rows = returned.reshape(row_count, full_width)
    gated = query_rows.astype(jnp.float32) * (convolved_rows + skip_gain[None, :] * signal)
    return gated.astype(jnp.bfloat16)


MESH = pl.DeviceIdType.MESH
LANES = 128


def split_bf16(values):
    high = values.astype(ml_dtypes.bfloat16)
    low = (values - high.astype(np.float64)).astype(ml_dtypes.bfloat16)
    return high, low


def block_transforms(block):
    order = np.concatenate([np.arange(0, block, 2), np.arange(1, block, 2)])
    phase = np.pi / block * (order[:, None] + 0.5) * np.arange(block)[None, :]
    forward = np.concatenate([np.cos(phase), -np.sin(phase)], axis=0)
    inverse = np.concatenate([np.cos(phase).T, -np.sin(phase).T], axis=1) / block
    forward_high, forward_low = split_bf16(forward)
    inverse_high, inverse_low = split_bf16(inverse)
    return (
        np.concatenate([forward_high, forward_high, forward_low], axis=1),
        np.concatenate([inverse_high, inverse_high, inverse_low], axis=1),
    )


def three_parts(values):
    high = values.astype(jnp.bfloat16)
    low = (values - high.astype(jnp.float32)).astype(jnp.bfloat16)
    return jnp.concatenate([high, low, high], axis=0)


def conv_kernel(
    seq_count,
    group_count,
    key_ref,
    value_ref,
    taps_ref,
    query_ref,
    gain_ref,
    forward_hbm,
    inverse_hbm,
    out_ref,
    signal,
    signal_in,
    taps_in,
    conv,
    conv_in,
    spectra,
    windows,
    product,
    forward_mat,
    inverse_mat,
    send_sem,
    signal_sem,
    taps_sem,
    conv_sem,
    const_sem,
):
    position = lax.axis_index("seq")
    group = lax.axis_index("ch")
    peers = seq_count * group_count
    me = position * group_count + group
    rows = key_ref.shape[0]
    block = rows * group_count
    half = block // 2

    def peer_of(step):
        there = lax.rem(position + step // group_count, seq_count)
        across = lax.rem(group + lax.rem(step, group_count), group_count)
        return there, across

    barrier = pltpu.get_barrier_semaphore()

    def greet(step, carry):
        pl.semaphore_signal(barrier, inc=1, device_id=peer_of(step), device_id_type=MESH)
        return carry

    lax.fori_loop(1, peers, greet, 0)
    load_forward = pltpu.make_async_copy(forward_hbm, forward_mat, const_sem.at[0])
    load_inverse = pltpu.make_async_copy(inverse_hbm, inverse_mat, const_sem.at[1])
    load_forward.start()
    load_inverse.start()
    signal[...] = key_ref[...].astype(jnp.float32) * value_ref[...].astype(jnp.float32)
    pl.semaphore_wait(barrier, peers - 1)

    my_rows = pl.ds(pl.multiple_of(me * rows, rows), rows)
    my_lanes = pl.ds(pl.multiple_of(me * LANES, LANES), LANES)

    def send(step, carry):
        there, across = peer_of(step)
        peer = there * group_count + across
        lanes = pl.ds(pl.multiple_of(peer * LANES, LANES), LANES)
        pltpu.make_async_remote_copy(
            src_ref=signal.at[:, lanes],
            dst_ref=signal_in.at[my_rows, :],
            send_sem=send_sem.at[0],
            recv_sem=signal_sem.at[position],
            device_id=(there, across),
            device_id_type=MESH,
        ).start()
        pltpu.make_async_remote_copy(
            src_ref=taps_ref.at[:, lanes],
            dst_ref=taps_in.at[my_rows, :],
            send_sem=send_sem.at[1],
            recv_sem=taps_sem.at[position],
            device_id=(there, across),
            device_id_type=MESH,
        ).start()
        return carry

    lax.fori_loop(1, peers, send, 0)
    pltpu.make_async_copy(
        signal.at[:, my_lanes], signal_in.at[my_rows, :], signal_sem.at[position]
    ).start()
    pltpu.make_async_copy(
        taps_ref.at[:, my_lanes], taps_in.at[my_rows, :], taps_sem.at[position]
    ).start()
    load_forward.wait()
    load_inverse.wait()

    for d in range(seq_count):
        here = pl.ds(d * block, block)
        pltpu.make_async_copy(signal_in.at[here, :], signal_in.at[here, :], signal_sem.at[d]).wait()
        pltpu.make_async_copy(taps_in.at[here, :], taps_in.at[here, :], taps_sem.at[d]).wait()
        both = jnp.concatenate([signal_in[here, :], taps_in[here, :]], axis=1)
        spectrum = jnp.dot(
            forward_mat[...], three_parts(both), preferred_element_type=jnp.float32
        )
        spectra[d] = spectrum[:, :LANES]
        tap_spectrum = spectrum[:, LANES:]
        if d == 0:
            windows[0] = tap_spectrum
        else:
            windows[d] += tap_spectrum
        if d + 1 < seq_count:
            windows[d + 1, 0:half] = -tap_spectrum[block : block + half]
            windows[d + 1, half:block] = tap_spectrum[block + half :]
            windows[d + 1, block : block + half] = tap_spectrum[0:half]
            windows[d + 1, block + half :] = -tap_spectrum[half:block]

        def multiply(chunk, carry):
            real = pl.ds(pl.multiple_of(chunk * 32, 32), 32)
            imag = pl.ds(pl.multiple_of(block + chunk * 32, 32), 32)
            total_real = jnp.zeros((32, LANES), jnp.float32)
            total_imag = jnp.zeros((32, LANES), jnp.float32)
            for j in range(d + 1):
                s_real = spectra[j, real, :]
                s_imag = spectra[j, imag, :]
                f_real = windows[d - j, real, :]
                f_imag = windows[d - j, imag, :]
                total_real += s_real * f_real - s_imag * f_imag
                total_imag += s_real * f_imag + s_imag * f_real
            product[real, :] = total_real
            product[imag, :] = total_imag
            return carry

        lax.fori_loop(0, block // 32, multiply, 0)
        conv[here, :] = jnp.dot(
            inverse_mat[...], three_parts(product[...]), preferred_element_type=jnp.float32
        )
        for c in range(group_count):
            owner = d * group_count + c
            piece = conv.at[pl.ds(owner * rows, rows), :]

            @pl.when(owner != me)
            def _():
                pltpu.make_async_remote_copy(
                    src_ref=piece,
                    dst_ref=conv_in.at[:, my_lanes],
                    send_sem=send_sem.at[2],
                    recv_sem=conv_sem.at[position],
                    device_id=(d, c),
                    device_id_type=MESH,
                ).start()

            @pl.when(owner == me)
            def _():
                pltpu.make_async_copy(piece, conv_in.at[:, my_lanes], conv_sem.at[position]).start()

    width = group_count * LANES
    for d in range(seq_count):
        lanes = pl.ds(d * width, width)
        pltpu.make_async_copy(conv_in.at[:, lanes], conv_in.at[:, lanes], conv_sem.at[d]).wait()
        skipped = gain_ref[0:1, lanes] * signal[:, lanes]
        out_ref[:, lanes] = (
            query_ref[:, lanes].astype(jnp.float32) * (conv_in[:, lanes] + skipped)
        ).astype(jnp.bfloat16)

    sent = pl.ds(0, (peers - 1) * rows)
    for which in range(3):
        pltpu.make_async_copy(
            signal_in.at[sent, :], signal_in.at[sent, :], send_sem.at[which]
        ).wait()


def fused_shards(query_rows, key_rows, value_rows, filter_taps, skip_gain):
    seq_count = lax.axis_size("seq")
    group_count = lax.axis_size("ch")
    rows, full_width = key_rows.shape
    block = rows * group_count
    tokens = block * seq_count
    forward, inverse = block_transforms(block)
    in_vmem = pl.BlockSpec(memory_space=pltpu.VMEM)
    in_any = pl.BlockSpec(memory_space=pl.ANY)
    return pl.pallas_call(
        functools.partial(conv_kernel, seq_count, group_count),
        out_shape=jax.ShapeDtypeStruct((rows, full_width), jnp.bfloat16),
        in_specs=[in_vmem] * 5 + [in_any] * 2,
        out_specs=in_vmem,
        scratch_shapes=[
            pltpu.VMEM((rows, full_width), jnp.float32),
            pltpu.VMEM((tokens, LANES), jnp.float32),
            pltpu.VMEM((tokens, LANES), jnp.float32),
            pltpu.VMEM((tokens, LANES), jnp.float32),
            pltpu.VMEM((rows, full_width), jnp.float32),
            pltpu.VMEM((seq_count, 2 * block, LANES), jnp.float32),
            pltpu.VMEM((seq_count, 2 * block, LANES), jnp.float32),
            pltpu.VMEM((2 * block, LANES), jnp.float32),
            pltpu.VMEM(forward.shape, jnp.bfloat16),
            pltpu.VMEM(inverse.shape, jnp.bfloat16),
            pltpu.SemaphoreType.DMA((3,)),
            pltpu.SemaphoreType.DMA((seq_count,)),
            pltpu.SemaphoreType.DMA((seq_count,)),
            pltpu.SemaphoreType.DMA((seq_count,)),
            pltpu.SemaphoreType.DMA((2,)),
        ],
        compiler_params=pltpu.CompilerParams(
            collective_id=0, has_side_effects=True, vmem_limit_bytes=48 * 1024 * 1024
        ),
    )(
        key_rows,
        value_rows,
        filter_taps,
        query_rows,
        skip_gain.reshape(1, full_width),
        jnp.asarray(forward),
        jnp.asarray(inverse),
    )


def solution(mesh):
    device_count = mesh.shape["seq"] * mesh.shape["ch"]
    in_specs = (
        P(("seq", "ch"), None),
        P(("seq", "ch"), None),
        P(("seq", "ch"), None),
        P(("seq", "ch"), None),
        P(),
    )
    out_specs = P(("seq", "ch"), None)

    def program(query_rows, key_rows, value_rows, filter_taps, skip_gain):
        tokens, channels = key_rows.shape
        one_tile_each = channels == LANES * device_count
        tiled_rows = tokens % (16 * device_count) == 0
        body = fused_shards if one_tile_each and tiled_rows else staged_shards
        return jax.shard_map(
            body, mesh=mesh, in_specs=in_specs, out_specs=out_specs, check_vma=False
        )(query_rows, key_rows, value_rows, filter_taps, skip_gain)

    return program
```

```python
import functools
import math

import jax
import jax.numpy as jnp
import ml_dtypes
import numpy as np
from jax import lax
from jax.experimental import pallas as pl
from jax.experimental.pallas import tpu as pltpu
from jax.sharding import PartitionSpec as P

highest = lax.Precision.HIGHEST


def angles(product_ids, modulus):
    return 2.0 * math.pi / modulus * (product_ids % modulus).astype(jnp.float32)


def contract(pattern, weights, operand):
    return jnp.einsum(
        pattern, weights, operand, precision=highest, preferred_element_type=jnp.float32
    )


def staged_shards(query_rows, key_rows, value_rows, filter_taps, skip_gain):
    seq_count = lax.axis_size("seq")
    group_count = lax.axis_size("ch")
    position = lax.axis_index("seq")
    row_count, full_width = key_rows.shape
    per_peer = row_count // seq_count
    columns = full_width // group_count
    local_rows = group_count * per_peer
    tokens = row_count * group_count
    slot_count = 2 * seq_count
    length = 2 * tokens * seq_count
    signal = key_rows.astype(jnp.float32) * value_rows.astype(jnp.float32)
    layout = (1, seq_count, 1, per_peer, full_width)
    moved_signal, moved_filter = (
        lax.all_to_all(
            lax.all_to_all(signal.reshape(layout), "seq", split_axis=1, concat_axis=0, tiled=True),
            "ch",
            split_axis=4,
            concat_axis=2,
            tiled=True,
        ),
        lax.all_to_all(
            lax.all_to_all(
                filter_taps.reshape(layout), "seq", split_axis=1, concat_axis=0, tiled=True
            ),
            "ch",
            split_axis=4,
            concat_axis=2,
            tiled=True,
        ),
    )
    moved_signal = moved_signal.reshape(seq_count, local_rows, columns)
    moved_filter = moved_filter.reshape(seq_count, local_rows, columns)
    slot_ids = jnp.arange(slot_count, dtype=jnp.int32)
    owners = slot_ids // 2
    freq_slot = jnp.where(
        slot_ids % 2 == 0, owners, jnp.where(owners == 0, seq_count, slot_count - owners)
    )
    blocks = jnp.arange(seq_count, dtype=jnp.int32)
    block_phase = angles(freq_slot[:, None] * blocks[None, :], slot_count)
    block_cos = jnp.cos(block_phase)
    block_sin = jnp.sin(block_phase)
    local_ids = jnp.arange(local_rows, dtype=jnp.int32)
    local_time = local_ids // per_peer * row_count + position * per_peer + local_ids % per_peer
    twist_angle = -angles(freq_slot[:, None] * local_time[None, :], length)
    twist_cos = jnp.cos(twist_angle)[:, :, None]
    twist_sin = jnp.sin(twist_angle)[:, :, None]

    def forward_blocks(real_part):
        out_real = contract("jd,dmc->jmc", block_cos, real_part)
        out_imag = -contract("jd,dmc->jmc", block_sin, real_part)
        return jnp.stack(
            [
                out_real * twist_cos - out_imag * twist_sin,
                out_real * twist_sin + out_imag * twist_cos,
            ]
        )

    all_ids = jnp.arange(tokens, dtype=jnp.int32)
    peer_id = all_ids // local_rows
    within = all_ids % local_rows
    all_time = within // per_peer * row_count + peer_id * per_peer + within % per_peer
    inner_phase = angles(all_ids[:, None] * all_time[None, :], tokens)
    inner_cos = jnp.cos(inner_phase)
    inner_sin = jnp.sin(inner_phase)

    def forward_inner(spectrum):
        real_part = spectrum[0]
        imag_part = spectrum[1]
        out_real = contract("qp,jpc->jqc", inner_cos, real_part) + contract(
            "qp,jpc->jqc", inner_sin, imag_part
        )
        out_imag = contract("qp,jpc->jqc", inner_cos, imag_part) - contract(
            "qp,jpc->jqc", inner_sin, real_part
        )
        return (out_real, out_imag)

    signal_spectrum, filter_spectrum = (
        lax.all_to_all(
            forward_blocks(moved_signal), "seq", split_axis=1, concat_axis=2, tiled=True
        ),
        lax.all_to_all(
            forward_blocks(moved_filter), "seq", split_axis=1, concat_axis=2, tiled=True
        ),
    )
    signal_real, signal_imag = forward_inner(signal_spectrum)
    filter_real, filter_imag = forward_inner(filter_spectrum)
    product_real = signal_real * filter_real - signal_imag * filter_imag
    product_imag = signal_real * filter_imag + signal_imag * filter_real
    back_real = contract("qp,jqc->jpc", inner_cos, product_real) - contract(
        "qp,jqc->jpc", inner_sin, product_imag
    )
    back_imag = contract("qp,jqc->jpc", inner_cos, product_imag) + contract(
        "qp,jqc->jpc", inner_sin, product_real
    )
    my_slots = jnp.stack([position, jnp.where(position == 0, seq_count, slot_count - position)])
    back_phase = angles(my_slots[:, None] * all_time[None, :], length)[:, :, None]
    back_cos = jnp.cos(back_phase)
    back_sin = jnp.sin(back_phase)
    turned_real = back_real * back_cos - back_imag * back_sin
    turned_imag = back_real * back_sin + back_imag * back_cos
    inverse_scale = 1.0 / length
    gathered = lax.all_to_all(
        jnp.stack([turned_real, turned_imag]), "seq", split_axis=2, concat_axis=1, tiled=True
    )
    convolved = (
        contract("jd,jmc->dmc", block_cos, gathered[0])
        - contract("jd,jmc->dmc", block_sin, gathered[1])
    ) * inverse_scale
    returned = lax.all_to_all(
        lax.all_to_all(
            convolved.reshape(seq_count, 1, group_count, per_peer, columns),
            "seq",
            split_axis=0,
            concat_axis=1,
            tiled=True,
        ),
        "ch",
        split_axis=2,
        concat_axis=4,
        tiled=True,
    )
    convolved_rows = returned.reshape(row_count, full_width)
    gated = query_rows.astype(jnp.float32) * (convolved_rows + skip_gain[None, :] * signal)
    return gated.astype(jnp.bfloat16)


MESH = pl.DeviceIdType.MESH
LANES = 128


def split_bf16(values):
    high = values.astype(ml_dtypes.bfloat16)
    low = (values - high.astype(np.float64)).astype(ml_dtypes.bfloat16)
    return high, low


def block_transforms(block):
    order = np.concatenate([np.arange(0, block, 2), np.arange(1, block, 2)])
    phase = np.pi / block * (order[:, None] + 0.5) * np.arange(block)[None, :]
    forward = np.concatenate([np.cos(phase), -np.sin(phase)], axis=0)
    inverse = np.concatenate([np.cos(phase).T, -np.sin(phase).T], axis=1) / block
    forward_high, forward_low = split_bf16(forward)
    inverse_high, inverse_low = split_bf16(inverse)
    return (
        np.concatenate([forward_high, forward_high, forward_low], axis=1),
        np.concatenate([inverse_high, inverse_high, inverse_low], axis=1),
    )


def three_parts(values):
    high = values.astype(jnp.bfloat16)
    low = (values - high.astype(jnp.float32)).astype(jnp.bfloat16)
    return jnp.concatenate([high, low, high], axis=0)


def conv_kernel(
    seq_count,
    group_count,
    key_hbm,
    value_hbm,
    taps_hbm,
    query_hbm,
    gain_hbm,
    forward_hbm,
    inverse_hbm,
    out_ref,
    key_ref,
    value_ref,
    query_ref,
    gain_ref,
    signal,
    signal_in,
    taps_in,
    conv,
    conv_in,
    spectra,
    windows,
    product,
    forward_mat,
    inverse_mat,
    send_sem,
    signal_sem,
    taps_sem,
    conv_sem,
    load_sem,
):
    position = lax.axis_index("seq")
    group = lax.axis_index("ch")
    peers = seq_count * group_count
    me = position * group_count + group
    rows = key_ref.shape[0]
    block = rows * group_count
    half = block // 2
    half_seq = seq_count // 2
    upper = position // half_seq
    turns = 2 if group_count % 2 == 0 else 1
    per_turn = group_count // turns

    loads = [
        pltpu.make_async_copy(source, target, load_sem.at[n])
        for n, (source, target) in enumerate(
            [
                (key_hbm, key_ref),
                (value_hbm, value_ref),
                (forward_hbm, forward_mat),
                (inverse_hbm, inverse_mat),
                (query_hbm, query_ref),
                (gain_hbm, gain_ref),
            ]
        )
    ]
    loads[0].start()
    loads[1].start()
    barrier = pltpu.get_barrier_semaphore()

    def greet(step, carry):
        there = lax.rem(position + step // group_count, seq_count)
        across = lax.rem(group + lax.rem(step, group_count), group_count)
        pl.semaphore_signal(barrier, inc=1, device_id=(there, across), device_id_type=MESH)
        return carry

    lax.fori_loop(1, peers, greet, 0)
    loads[0].wait()
    loads[1].wait()
    signal[...] = key_ref[...].astype(jnp.float32) * value_ref[...].astype(jnp.float32)
    for load in loads[2:]:
        load.start()
    pl.semaphore_wait(barrier, peers - 1)

    my_rows = pl.ds(pl.multiple_of(me * rows, rows), rows)
    my_lanes = pl.ds(pl.multiple_of(me * LANES, LANES), LANES)

    def send(step, carry):
        turn = step // (seq_count * per_turn)
        inner = lax.rem(step, seq_count * per_turn)
        hop = inner // per_turn
        across = turns * lax.rem(group // turns + lax.rem(inner, per_turn), per_turn) + turn
        side = lax.rem(upper + 1 + lax.rem(hop, 2), 2)
        there = side * half_seq + lax.rem(position + hop // 2, half_seq)
        peer = there * group_count + across
        lanes = pl.ds(pl.multiple_of(peer * LANES, LANES), LANES)

        @pl.when(peer != me)
        def _():
            pltpu.make_async_remote_copy(
                src_ref=taps_hbm.at[:, lanes],
                dst_ref=taps_in.at[my_rows, :],
                send_sem=send_sem.at[1],
                recv_sem=taps_sem.at[position],
                device_id=(there, across),
                device_id_type=MESH,
            ).start()
            pltpu.make_async_remote_copy(
                src_ref=signal.at[:, lanes],
                dst_ref=signal_in.at[my_rows, :],
                send_sem=send_sem.at[0],
                recv_sem=signal_sem.at[position],
                device_id=(there, across),
                device_id_type=MESH,
            ).start()

        return carry

    pltpu.make_async_copy(
        signal.at[:, my_lanes], signal_in.at[my_rows, :], signal_sem.at[position]
    ).start()
    pltpu.make_async_copy(
        taps_hbm.at[:, my_lanes], taps_in.at[my_rows, :], taps_sem.at[position]
    ).start()
    lax.fori_loop(0, peers, send, 0)
    for load in loads[2:]:
        load.wait()

    def transform(d, carry):
        here = pl.ds(pl.multiple_of(d * block, block), block)
        pltpu.make_async_copy(signal_in.at[here, :], signal_in.at[here, :], signal_sem.at[d]).wait()
        pltpu.make_async_copy(taps_in.at[here, :], taps_in.at[here, :], taps_sem.at[d]).wait()
        both = jnp.concatenate([signal_in[here, :], taps_in[here, :]], axis=1)
        spectrum = jnp.dot(
            forward_mat[...], three_parts(both), preferred_element_type=jnp.float32
        )
        spectra[d] = spectrum[:, :LANES]
        tap_spectrum = spectrum[:, LANES:]
        windows[d] += tap_spectrum
        windows[d + 1, 0:half] = -tap_spectrum[block : block + half]
        windows[d + 1, half:block] = tap_spectrum[block + half :]
        windows[d + 1, block : block + half] = tap_spectrum[0:half]
        windows[d + 1, block + half :] = -tap_spectrum[half:block]
        return carry

    chunk_rows = 64

    def output(d, carry):
        for chunk in range(block // chunk_rows):
            real = pl.ds(chunk * chunk_rows, chunk_rows)
            imag = pl.ds(block + chunk * chunk_rows, chunk_rows)

            def pair(j, totals):
                s_real = spectra[j, real, :]
                s_imag = spectra[j, imag, :]
                f_real = windows[d - j, real, :]
                f_imag = windows[d - j, imag, :]
                return (
                    totals[0] + (s_real * f_real - s_imag * f_imag),
                    totals[1] + (s_real * f_imag + s_imag * f_real),
                )

            zero = jnp.zeros((chunk_rows, LANES), jnp.float32)
            product[real, :], product[imag, :] = lax.fori_loop(0, d + 1, pair, (zero, zero))
        here = pl.ds(pl.multiple_of(d * block, block), block)
        conv[here, :] = jnp.dot(
            inverse_mat[...], three_parts(product[...]), preferred_element_type=jnp.float32
        )
        for c in range(group_count):
            owner = d * group_count + c
            piece = conv.at[pl.ds(pl.multiple_of(owner * rows, rows), rows), :]

            @pl.when(owner != me)
            def _():
                pltpu.make_async_remote_copy(
                    src_ref=piece,
                    dst_ref=conv_in.at[:, my_lanes],
                    send_sem=send_sem.at[2],
                    recv_sem=conv_sem.at[position],
                    device_id=(d, c),
                    device_id_type=MESH,
                ).start()

            @pl.when(owner == me)
            def _():
                pltpu.make_async_copy(piece, conv_in.at[:, my_lanes], conv_sem.at[position]).start()

        return carry

    windows[0] = jnp.zeros((2 * block, LANES), jnp.float32)
    lax.fori_loop(0, half_seq, transform, 0)
    lax.fori_loop(0, half_seq * upper, output, 0)
    lax.fori_loop(half_seq, seq_count, transform, 0)
    lax.fori_loop(half_seq, seq_count, output, 0)
    lax.fori_loop(0, half_seq * (1 - upper), output, 0)

    width = group_count * LANES

    def finish(d, carry):
        lanes = pl.ds(pl.multiple_of(d * width, width), width)
        pltpu.make_async_copy(conv_in.at[:, lanes], conv_in.at[:, lanes], conv_sem.at[d]).wait()
        skipped = gain_ref[0:1, lanes] * signal[:, lanes]
        out_ref[:, lanes] = (
            query_ref[:, lanes].astype(jnp.float32) * (conv_in[:, lanes] + skipped)
        ).astype(jnp.bfloat16)
        return carry

    lax.fori_loop(0, seq_count, finish, 0)

    sent = pl.ds(0, (peers - 1) * rows)
    for which in range(3):
        pltpu.make_async_copy(
            signal_in.at[sent, :], signal_in.at[sent, :], send_sem.at[which]
        ).wait()


def fused_shards(query_rows, key_rows, value_rows, filter_taps, skip_gain):
    seq_count = lax.axis_size("seq")
    group_count = lax.axis_size("ch")
    rows, full_width = key_rows.shape
    block = rows * group_count
    tokens = block * seq_count
    forward, inverse = block_transforms(block)
    in_vmem = pl.BlockSpec(memory_space=pltpu.VMEM)
    in_hbm = pl.BlockSpec(memory_space=pltpu.HBM)
    return pl.pallas_call(
        functools.partial(conv_kernel, seq_count, group_count),
        out_shape=jax.ShapeDtypeStruct((rows, full_width), jnp.bfloat16),
        in_specs=[in_hbm] * 7,
        out_specs=in_vmem,
        scratch_shapes=[
            pltpu.VMEM((rows, full_width), jnp.bfloat16),
            pltpu.VMEM((rows, full_width), jnp.bfloat16),
            pltpu.VMEM((rows, full_width), jnp.bfloat16),
            pltpu.VMEM((1, full_width), jnp.float32),
            pltpu.VMEM((rows, full_width), jnp.float32),
            pltpu.VMEM((tokens, LANES), jnp.float32),
            pltpu.VMEM((tokens, LANES), jnp.float32),
            pltpu.VMEM((tokens, LANES), jnp.float32),
            pltpu.VMEM((rows, full_width), jnp.float32),
            pltpu.VMEM((seq_count, 2 * block, LANES), jnp.float32),
            pltpu.VMEM((seq_count + 1, 2 * block, LANES), jnp.float32),
            pltpu.VMEM((2 * block, LANES), jnp.float32),
            pltpu.VMEM(forward.shape, jnp.bfloat16),
            pltpu.VMEM(inverse.shape, jnp.bfloat16),
            pltpu.SemaphoreType.DMA((3,)),
            pltpu.SemaphoreType.DMA((seq_count,)),
            pltpu.SemaphoreType.DMA((seq_count,)),
            pltpu.SemaphoreType.DMA((seq_count,)),
            pltpu.SemaphoreType.DMA((6,)),
        ],
        compiler_params=pltpu.CompilerParams(
            collective_id=0, has_side_effects=True, vmem_limit_bytes=127 * 512 * 1024
        ),
    )(
        key_rows,
        value_rows,
        filter_taps,
        query_rows,
        skip_gain.reshape(1, full_width),
        jnp.asarray(forward),
        jnp.asarray(inverse),
    )


def solution(mesh):
    device_count = mesh.shape["seq"] * mesh.shape["ch"]
    in_specs = (
        P(("seq", "ch"), None),
        P(("seq", "ch"), None),
        P(("seq", "ch"), None),
        P(("seq", "ch"), None),
        P(),
    )
    out_specs = P(("seq", "ch"), None)

    def program(query_rows, key_rows, value_rows, filter_taps, skip_gain):
        tokens, channels = key_rows.shape
        one_tile_each = channels == LANES * device_count and mesh.shape["seq"] % 2 == 0
        tiled_rows = tokens % (16 * device_count) == 0
        body = fused_shards if one_tile_each and tiled_rows else staged_shards
        return jax.shard_map(
            body, mesh=mesh, in_specs=in_specs, out_specs=out_specs, check_vma=False
        )(query_rows, key_rows, value_rows, filter_taps, skip_gain)

    return program
```

```python
import functools
import math

import jax
import jax.numpy as jnp
import ml_dtypes
import numpy as np
from jax import lax
from jax.experimental import pallas as pl
from jax.experimental.pallas import tpu as pltpu
from jax.sharding import PartitionSpec as P

highest = lax.Precision.HIGHEST


def angles(product_ids, modulus):
    return 2.0 * math.pi / modulus * (product_ids % modulus).astype(jnp.float32)


def contract(pattern, weights, operand):
    return jnp.einsum(
        pattern, weights, operand, precision=highest, preferred_element_type=jnp.float32
    )


def staged_shards(query_rows, key_rows, value_rows, filter_taps, skip_gain):
    seq_count = lax.axis_size("seq")
    group_count = lax.axis_size("ch")
    position = lax.axis_index("seq")
    row_count, full_width = key_rows.shape
    per_peer = row_count // seq_count
    columns = full_width // group_count
    local_rows = group_count * per_peer
    tokens = row_count * group_count
    slot_count = 2 * seq_count
    length = 2 * tokens * seq_count
    signal = key_rows.astype(jnp.float32) * value_rows.astype(jnp.float32)
    layout = (1, seq_count, 1, per_peer, full_width)
    moved_signal, moved_filter = (
        lax.all_to_all(
            lax.all_to_all(signal.reshape(layout), "seq", split_axis=1, concat_axis=0, tiled=True),
            "ch",
            split_axis=4,
            concat_axis=2,
            tiled=True,
        ),
        lax.all_to_all(
            lax.all_to_all(
                filter_taps.reshape(layout), "seq", split_axis=1, concat_axis=0, tiled=True
            ),
            "ch",
            split_axis=4,
            concat_axis=2,
            tiled=True,
        ),
    )
    moved_signal = moved_signal.reshape(seq_count, local_rows, columns)
    moved_filter = moved_filter.reshape(seq_count, local_rows, columns)
    slot_ids = jnp.arange(slot_count, dtype=jnp.int32)
    owners = slot_ids // 2
    freq_slot = jnp.where(
        slot_ids % 2 == 0, owners, jnp.where(owners == 0, seq_count, slot_count - owners)
    )
    blocks = jnp.arange(seq_count, dtype=jnp.int32)
    block_phase = angles(freq_slot[:, None] * blocks[None, :], slot_count)
    block_cos = jnp.cos(block_phase)
    block_sin = jnp.sin(block_phase)
    local_ids = jnp.arange(local_rows, dtype=jnp.int32)
    local_time = local_ids // per_peer * row_count + position * per_peer + local_ids % per_peer
    twist_angle = -angles(freq_slot[:, None] * local_time[None, :], length)
    twist_cos = jnp.cos(twist_angle)[:, :, None]
    twist_sin = jnp.sin(twist_angle)[:, :, None]

    def forward_blocks(real_part):
        out_real = contract("jd,dmc->jmc", block_cos, real_part)
        out_imag = -contract("jd,dmc->jmc", block_sin, real_part)
        return jnp.stack(
            [
                out_real * twist_cos - out_imag * twist_sin,
                out_real * twist_sin + out_imag * twist_cos,
            ]
        )

    all_ids = jnp.arange(tokens, dtype=jnp.int32)
    peer_id = all_ids // local_rows
    within = all_ids % local_rows
    all_time = within // per_peer * row_count + peer_id * per_peer + within % per_peer
    inner_phase = angles(all_ids[:, None] * all_time[None, :], tokens)
    inner_cos = jnp.cos(inner_phase)
    inner_sin = jnp.sin(inner_phase)

    def forward_inner(spectrum):
        real_part = spectrum[0]
        imag_part = spectrum[1]
        out_real = contract("qp,jpc->jqc", inner_cos, real_part) + contract(
            "qp,jpc->jqc", inner_sin, imag_part
        )
        out_imag = contract("qp,jpc->jqc", inner_cos, imag_part) - contract(
            "qp,jpc->jqc", inner_sin, real_part
        )
        return (out_real, out_imag)

    signal_spectrum, filter_spectrum = (
        lax.all_to_all(
            forward_blocks(moved_signal), "seq", split_axis=1, concat_axis=2, tiled=True
        ),
        lax.all_to_all(
            forward_blocks(moved_filter), "seq", split_axis=1, concat_axis=2, tiled=True
        ),
    )
    signal_real, signal_imag = forward_inner(signal_spectrum)
    filter_real, filter_imag = forward_inner(filter_spectrum)
    product_real = signal_real * filter_real - signal_imag * filter_imag
    product_imag = signal_real * filter_imag + signal_imag * filter_real
    back_real = contract("qp,jqc->jpc", inner_cos, product_real) - contract(
        "qp,jqc->jpc", inner_sin, product_imag
    )
    back_imag = contract("qp,jqc->jpc", inner_cos, product_imag) + contract(
        "qp,jqc->jpc", inner_sin, product_real
    )
    my_slots = jnp.stack([position, jnp.where(position == 0, seq_count, slot_count - position)])
    back_phase = angles(my_slots[:, None] * all_time[None, :], length)[:, :, None]
    back_cos = jnp.cos(back_phase)
    back_sin = jnp.sin(back_phase)
    turned_real = back_real * back_cos - back_imag * back_sin
    turned_imag = back_real * back_sin + back_imag * back_cos
    inverse_scale = 1.0 / length
    gathered = lax.all_to_all(
        jnp.stack([turned_real, turned_imag]), "seq", split_axis=2, concat_axis=1, tiled=True
    )
    convolved = (
        contract("jd,jmc->dmc", block_cos, gathered[0])
        - contract("jd,jmc->dmc", block_sin, gathered[1])
    ) * inverse_scale
    returned = lax.all_to_all(
        lax.all_to_all(
            convolved.reshape(seq_count, 1, group_count, per_peer, columns),
            "seq",
            split_axis=0,
            concat_axis=1,
            tiled=True,
        ),
        "ch",
        split_axis=2,
        concat_axis=4,
        tiled=True,
    )
    convolved_rows = returned.reshape(row_count, full_width)
    gated = query_rows.astype(jnp.float32) * (convolved_rows + skip_gain[None, :] * signal)
    return gated.astype(jnp.bfloat16)


MESH = pl.DeviceIdType.MESH
LANES = 128


def split_bf16(values):
    high = values.astype(ml_dtypes.bfloat16)
    low = (values - high.astype(np.float64)).astype(ml_dtypes.bfloat16)
    return high, low


def block_transforms(block):
    order = np.concatenate([np.arange(0, block, 2), np.arange(1, block, 2)])
    phase = np.pi / block * (order[:, None] + 0.5) * np.arange(block)[None, :]
    forward = np.concatenate([np.cos(phase), -np.sin(phase)], axis=0)
    inverse = np.concatenate([np.cos(phase).T, -np.sin(phase).T], axis=1) / block
    forward_high, forward_low = split_bf16(forward)
    inverse_high, inverse_low = split_bf16(inverse)
    return (
        np.concatenate([forward_high, forward_high, forward_low], axis=1),
        np.concatenate([inverse_high, inverse_high, inverse_low], axis=1),
    )


def three_parts(values):
    high = values.astype(jnp.bfloat16)
    low = (values - high.astype(jnp.float32)).astype(jnp.bfloat16)
    return jnp.concatenate([high, low, high], axis=0)


def conv_kernel(
    seq_count,
    group_count,
    key_hbm,
    value_hbm,
    taps_hbm,
    query_hbm,
    gain_hbm,
    forward_hbm,
    inverse_hbm,
    out_hbm,
    out_ref,
    key_ref,
    value_ref,
    query_ref,
    gain_ref,
    signal,
    signal_in,
    taps_in,
    conv,
    conv_in,
    spectra,
    windows,
    product,
    forward_mat,
    inverse_mat,
    send_sem,
    signal_sem,
    taps_sem,
    conv_sem,
    load_sem,
    store_sem,
):
    position = lax.axis_index("seq")
    group = lax.axis_index("ch")
    peers = seq_count * group_count
    me = position * group_count + group
    rows = key_ref.shape[0]
    block = rows * group_count
    half = block // 2
    half_seq = seq_count // 2
    upper = position // half_seq
    turns = 2 if group_count % 2 == 0 else 1
    per_turn = group_count // turns

    loads = [
        pltpu.make_async_copy(source, target, load_sem.at[n])
        for n, (source, target) in enumerate(
            [
                (key_hbm, key_ref),
                (value_hbm, value_ref),
                (forward_hbm, forward_mat),
                (inverse_hbm, inverse_mat),
                (query_hbm, query_ref),
                (gain_hbm, gain_ref),
            ]
        )
    ]
    loads[0].start()
    loads[1].start()
    barrier = pltpu.get_barrier_semaphore()

    def greet(step, carry):
        there = lax.rem(position + step // group_count, seq_count)
        across = lax.rem(group + lax.rem(step, group_count), group_count)
        pl.semaphore_signal(barrier, inc=1, device_id=(there, across), device_id_type=MESH)
        return carry

    lax.fori_loop(1, peers, greet, 0)
    loads[0].wait()
    loads[1].wait()
    signal[...] = key_ref[...].astype(jnp.float32) * value_ref[...].astype(jnp.float32)
    for load in loads[2:]:
        load.start()
    pl.semaphore_wait(barrier, peers - 1)

    my_rows = pl.ds(pl.multiple_of(me * rows, rows), rows)
    my_lanes = pl.ds(pl.multiple_of(me * LANES, LANES), LANES)

    def send(step, carry):
        turn = step // (seq_count * per_turn)
        inner = lax.rem(step, seq_count * per_turn)
        hop = inner // per_turn
        across = turns * lax.rem(group // turns + lax.rem(inner, per_turn), per_turn) + turn
        side = lax.rem(upper + 1 + lax.rem(hop, 2), 2)
        there = side * half_seq + lax.rem(position + hop // 2, half_seq)
        peer = there * group_count + across
        lanes = pl.ds(pl.multiple_of(peer * LANES, LANES), LANES)

        @pl.when(peer != me)
        def _():
            pltpu.make_async_remote_copy(
                src_ref=taps_hbm.at[:, lanes],
                dst_ref=taps_in.at[my_rows, :],
                send_sem=send_sem.at[1],
                recv_sem=taps_sem.at[position],
                device_id=(there, across),
                device_id_type=MESH,
            ).start()
            pltpu.make_async_remote_copy(
                src_ref=signal.at[:, lanes],
                dst_ref=signal_in.at[my_rows, :],
                send_sem=send_sem.at[0],
                recv_sem=signal_sem.at[position],
                device_id=(there, across),
                device_id_type=MESH,
            ).start()

        return carry

    pltpu.make_async_copy(
        signal.at[:, my_lanes], signal_in.at[my_rows, :], signal_sem.at[position]
    ).start()
    pltpu.make_async_copy(
        taps_hbm.at[:, my_lanes], taps_in.at[my_rows, :], taps_sem.at[position]
    ).start()
    lax.fori_loop(0, peers, send, 0)
    for load in loads[2:]:
        load.wait()

    def transform(d, carry):
        here = pl.ds(pl.multiple_of(d * block, block), block)
        pltpu.make_async_copy(signal_in.at[here, :], signal_in.at[here, :], signal_sem.at[d]).wait()
        pltpu.make_async_copy(taps_in.at[here, :], taps_in.at[here, :], taps_sem.at[d]).wait()
        both = jnp.concatenate([signal_in[here, :], taps_in[here, :]], axis=1)
        spectrum = jnp.dot(
            forward_mat[...], three_parts(both), preferred_element_type=jnp.float32
        )
        spectra[d] = spectrum[:, :LANES]
        tap_spectrum = spectrum[:, LANES:]
        windows[d] += tap_spectrum
        windows[d + 1, 0:half] = -tap_spectrum[block : block + half]
        windows[d + 1, half:block] = tap_spectrum[block + half :]
        windows[d + 1, block : block + half] = tap_spectrum[0:half]
        windows[d + 1, block + half :] = -tap_spectrum[half:block]
        return carry

    chunk_rows = 64

    def output(d, carry):
        for chunk in range(block // chunk_rows):
            real = pl.ds(chunk * chunk_rows, chunk_rows)
            imag = pl.ds(block + chunk * chunk_rows, chunk_rows)

            def pair(j, totals):
                s_real = spectra[j, real, :]
                s_imag = spectra[j, imag, :]
                f_real = windows[d - j, real, :]
                f_imag = windows[d - j, imag, :]
                return (
                    totals[0] + (s_real * f_real - s_imag * f_imag),
                    totals[1] + (s_real * f_imag + s_imag * f_real),
                )

            zero = jnp.zeros((chunk_rows, LANES), jnp.float32)
            product[real, :], product[imag, :] = lax.fori_loop(0, d + 1, pair, (zero, zero))
        here = pl.ds(pl.multiple_of(d * block, block), block)
        conv[here, :] = jnp.dot(
            inverse_mat[...], three_parts(product[...]), preferred_element_type=jnp.float32
        )
        for c in range(group_count):
            owner = d * group_count + c
            piece = conv.at[pl.ds(pl.multiple_of(owner * rows, rows), rows), :]

            @pl.when(owner != me)
            def _():
                pltpu.make_async_remote_copy(
                    src_ref=piece,
                    dst_ref=conv_in.at[:, my_lanes],
                    send_sem=send_sem.at[2],
                    recv_sem=conv_sem.at[position],
                    device_id=(d, c),
                    device_id_type=MESH,
                ).start()

            @pl.when(owner == me)
            def _():
                pltpu.make_async_copy(piece, conv_in.at[:, my_lanes], conv_sem.at[position]).start()

        return carry

    windows[0] = jnp.zeros((2 * block, LANES), jnp.float32)
    lax.fori_loop(0, half_seq, transform, 0)
    lax.fori_loop(0, half_seq * upper, output, 0)
    lax.fori_loop(half_seq, seq_count, transform, 0)
    lax.fori_loop(half_seq, seq_count * upper, output, 0)

    def alternate(i, carry):
        return output(half_seq * lax.rem(i + 1, 2) + i // 2, carry)

    lax.fori_loop(0, seq_count * (1 - upper), alternate, 0)

    width = group_count * LANES

    def finish(step, carry):
        d = lax.rem(step + half_seq * (1 - upper), seq_count)
        lanes = pl.ds(pl.multiple_of(d * width, width), width)
        pltpu.make_async_copy(conv_in.at[:, lanes], conv_in.at[:, lanes], conv_sem.at[d]).wait()
        skipped = gain_ref[0:1, lanes] * signal[:, lanes]
        out_ref[:, lanes] = (
            query_ref[:, lanes].astype(jnp.float32) * (conv_in[:, lanes] + skipped)
        ).astype(jnp.bfloat16)
        pltpu.make_async_copy(out_ref.at[:, lanes], out_hbm.at[:, lanes], store_sem.at[d]).start()
        return carry

    lax.fori_loop(0, seq_count, finish, 0)

    sent = pl.ds(0, (peers - 1) * rows)
    for which in range(3):
        pltpu.make_async_copy(
            signal_in.at[sent, :], signal_in.at[sent, :], send_sem.at[which]
        ).wait()
    for d in range(seq_count):
        lanes = pl.ds(d * width, width)
        pltpu.make_async_copy(out_ref.at[:, lanes], out_hbm.at[:, lanes], store_sem.at[d]).wait()


def fused_shards(query_rows, key_rows, value_rows, filter_taps, skip_gain):
    seq_count = lax.axis_size("seq")
    group_count = lax.axis_size("ch")
    rows, full_width = key_rows.shape
    block = rows * group_count
    tokens = block * seq_count
    forward, inverse = block_transforms(block)
    in_hbm = pl.BlockSpec(memory_space=pltpu.HBM)
    return pl.pallas_call(
        functools.partial(conv_kernel, seq_count, group_count),
        out_shape=jax.ShapeDtypeStruct((rows, full_width), jnp.bfloat16),
        in_specs=[in_hbm] * 7,
        out_specs=in_hbm,
        scratch_shapes=[
            pltpu.VMEM((rows, full_width), jnp.bfloat16),
            pltpu.VMEM((rows, full_width), jnp.bfloat16),
            pltpu.VMEM((rows, full_width), jnp.bfloat16),
            pltpu.VMEM((rows, full_width), jnp.bfloat16),
            pltpu.VMEM((1, full_width), jnp.float32),
            pltpu.VMEM((rows, full_width), jnp.float32),
            pltpu.VMEM((tokens, LANES), jnp.float32),
            pltpu.VMEM((tokens, LANES), jnp.float32),
            pltpu.VMEM((tokens, LANES), jnp.float32),
            pltpu.VMEM((rows, full_width), jnp.float32),
            pltpu.VMEM((seq_count, 2 * block, LANES), jnp.float32),
            pltpu.VMEM((seq_count + 1, 2 * block, LANES), jnp.float32),
            pltpu.VMEM((2 * block, LANES), jnp.float32),
            pltpu.VMEM(forward.shape, jnp.bfloat16),
            pltpu.VMEM(inverse.shape, jnp.bfloat16),
            pltpu.SemaphoreType.DMA((3,)),
            pltpu.SemaphoreType.DMA((seq_count,)),
            pltpu.SemaphoreType.DMA((seq_count,)),
            pltpu.SemaphoreType.DMA((seq_count,)),
            pltpu.SemaphoreType.DMA((6,)),
            pltpu.SemaphoreType.DMA((seq_count,)),
        ],
        compiler_params=pltpu.CompilerParams(
            collective_id=0, has_side_effects=True, vmem_limit_bytes=127 * 512 * 1024
        ),
    )(
        key_rows,
        value_rows,
        filter_taps,
        query_rows,
        skip_gain.reshape(1, full_width),
        jnp.asarray(forward),
        jnp.asarray(inverse),
    )


def solution(mesh):
    device_count = mesh.shape["seq"] * mesh.shape["ch"]
    in_specs = (
        P(("seq", "ch"), None),
        P(("seq", "ch"), None),
        P(("seq", "ch"), None),
        P(("seq", "ch"), None),
        P(),
    )
    out_specs = P(("seq", "ch"), None)

    def program(query_rows, key_rows, value_rows, filter_taps, skip_gain):
        tokens, channels = key_rows.shape
        one_tile_each = channels == LANES * device_count and mesh.shape["seq"] % 2 == 0
        tiled_rows = tokens % (16 * device_count) == 0
        body = fused_shards if one_tile_each and tiled_rows else staged_shards
        return jax.shard_map(
            body, mesh=mesh, in_specs=in_specs, out_specs=out_specs, check_vma=False
        )(query_rows, key_rows, value_rows, filter_taps, skip_gain)

    return program
```

```python
import functools
import math

import jax
import jax.numpy as jnp
import ml_dtypes
import numpy as np
from jax import lax
from jax.experimental import pallas as pl
from jax.experimental.pallas import tpu as pltpu
from jax.sharding import PartitionSpec as P

highest = lax.Precision.HIGHEST


def angles(product_ids, modulus):
    return 2.0 * math.pi / modulus * (product_ids % modulus).astype(jnp.float32)


def contract(pattern, weights, operand):
    return jnp.einsum(
        pattern, weights, operand, precision=highest, preferred_element_type=jnp.float32
    )


def staged_shards(query_rows, key_rows, value_rows, filter_taps, skip_gain):
    seq_count = lax.axis_size("seq")
    group_count = lax.axis_size("ch")
    position = lax.axis_index("seq")
    row_count, full_width = key_rows.shape
    per_peer = row_count // seq_count
    columns = full_width // group_count
    local_rows = group_count * per_peer
    tokens = row_count * group_count
    slot_count = 2 * seq_count
    length = 2 * tokens * seq_count
    signal = key_rows.astype(jnp.float32) * value_rows.astype(jnp.float32)
    layout = (1, seq_count, 1, per_peer, full_width)
    moved_signal, moved_filter = (
        lax.all_to_all(
            lax.all_to_all(signal.reshape(layout), "seq", split_axis=1, concat_axis=0, tiled=True),
            "ch",
            split_axis=4,
            concat_axis=2,
            tiled=True,
        ),
        lax.all_to_all(
            lax.all_to_all(
                filter_taps.reshape(layout), "seq", split_axis=1, concat_axis=0, tiled=True
            ),
            "ch",
            split_axis=4,
            concat_axis=2,
            tiled=True,
        ),
    )
    moved_signal = moved_signal.reshape(seq_count, local_rows, columns)
    moved_filter = moved_filter.reshape(seq_count, local_rows, columns)
    slot_ids = jnp.arange(slot_count, dtype=jnp.int32)
    owners = slot_ids // 2
    freq_slot = jnp.where(
        slot_ids % 2 == 0, owners, jnp.where(owners == 0, seq_count, slot_count - owners)
    )
    blocks = jnp.arange(seq_count, dtype=jnp.int32)
    block_phase = angles(freq_slot[:, None] * blocks[None, :], slot_count)
    block_cos = jnp.cos(block_phase)
    block_sin = jnp.sin(block_phase)
    local_ids = jnp.arange(local_rows, dtype=jnp.int32)
    local_time = local_ids // per_peer * row_count + position * per_peer + local_ids % per_peer
    twist_angle = -angles(freq_slot[:, None] * local_time[None, :], length)
    twist_cos = jnp.cos(twist_angle)[:, :, None]
    twist_sin = jnp.sin(twist_angle)[:, :, None]

    def forward_blocks(real_part):
        out_real = contract("jd,dmc->jmc", block_cos, real_part)
        out_imag = -contract("jd,dmc->jmc", block_sin, real_part)
        return jnp.stack(
            [
                out_real * twist_cos - out_imag * twist_sin,
                out_real * twist_sin + out_imag * twist_cos,
            ]
        )

    all_ids = jnp.arange(tokens, dtype=jnp.int32)
    peer_id = all_ids // local_rows
    within = all_ids % local_rows
    all_time = within // per_peer * row_count + peer_id * per_peer + within % per_peer
    inner_phase = angles(all_ids[:, None] * all_time[None, :], tokens)
    inner_cos = jnp.cos(inner_phase)
    inner_sin = jnp.sin(inner_phase)

    def forward_inner(spectrum):
        real_part = spectrum[0]
        imag_part = spectrum[1]
        out_real = contract("qp,jpc->jqc", inner_cos, real_part) + contract(
            "qp,jpc->jqc", inner_sin, imag_part
        )
        out_imag = contract("qp,jpc->jqc", inner_cos, imag_part) - contract(
            "qp,jpc->jqc", inner_sin, real_part
        )
        return (out_real, out_imag)

    signal_spectrum, filter_spectrum = (
        lax.all_to_all(
            forward_blocks(moved_signal), "seq", split_axis=1, concat_axis=2, tiled=True
        ),
        lax.all_to_all(
            forward_blocks(moved_filter), "seq", split_axis=1, concat_axis=2, tiled=True
        ),
    )
    signal_real, signal_imag = forward_inner(signal_spectrum)
    filter_real, filter_imag = forward_inner(filter_spectrum)
    product_real = signal_real * filter_real - signal_imag * filter_imag
    product_imag = signal_real * filter_imag + signal_imag * filter_real
    back_real = contract("qp,jqc->jpc", inner_cos, product_real) - contract(
        "qp,jqc->jpc", inner_sin, product_imag
    )
    back_imag = contract("qp,jqc->jpc", inner_cos, product_imag) + contract(
        "qp,jqc->jpc", inner_sin, product_real
    )
    my_slots = jnp.stack([position, jnp.where(position == 0, seq_count, slot_count - position)])
    back_phase = angles(my_slots[:, None] * all_time[None, :], length)[:, :, None]
    back_cos = jnp.cos(back_phase)
    back_sin = jnp.sin(back_phase)
    turned_real = back_real * back_cos - back_imag * back_sin
    turned_imag = back_real * back_sin + back_imag * back_cos
    inverse_scale = 1.0 / length
    gathered = lax.all_to_all(
        jnp.stack([turned_real, turned_imag]), "seq", split_axis=2, concat_axis=1, tiled=True
    )
    convolved = (
        contract("jd,jmc->dmc", block_cos, gathered[0])
        - contract("jd,jmc->dmc", block_sin, gathered[1])
    ) * inverse_scale
    returned = lax.all_to_all(
        lax.all_to_all(
            convolved.reshape(seq_count, 1, group_count, per_peer, columns),
            "seq",
            split_axis=0,
            concat_axis=1,
            tiled=True,
        ),
        "ch",
        split_axis=2,
        concat_axis=4,
        tiled=True,
    )
    convolved_rows = returned.reshape(row_count, full_width)
    gated = query_rows.astype(jnp.float32) * (convolved_rows + skip_gain[None, :] * signal)
    return gated.astype(jnp.bfloat16)


MESH = pl.DeviceIdType.MESH
LANES = 128


def split_bf16(values):
    high = values.astype(ml_dtypes.bfloat16)
    low = (values - high.astype(np.float64)).astype(ml_dtypes.bfloat16)
    return high, low


def block_transforms(block):
    order = np.concatenate([np.arange(0, block, 2), np.arange(1, block, 2)])
    phase = np.pi / block * (order[:, None] + 0.5) * np.arange(block)[None, :]
    forward = np.concatenate([np.cos(phase), -np.sin(phase)], axis=0)
    inverse = np.concatenate([np.cos(phase).T, -np.sin(phase).T], axis=1) / block
    forward_high, forward_low = split_bf16(forward)
    inverse_high, inverse_low = split_bf16(inverse)
    return (
        np.concatenate([forward_high, forward_high, forward_low], axis=1),
        np.concatenate([inverse_high, inverse_high, inverse_low], axis=1),
    )


def three_parts(values):
    high = values.astype(jnp.bfloat16)
    low = (values - high.astype(jnp.float32)).astype(jnp.bfloat16)
    return jnp.concatenate([high, low, high], axis=0)


def conv_kernel(
    seq_count,
    group_count,
    key_hbm,
    value_hbm,
    taps_hbm,
    query_hbm,
    gain_hbm,
    forward_hbm,
    inverse_hbm,
    out_ref,
    key_ref,
    value_ref,
    query_ref,
    gain_ref,
    signal,
    signal_in,
    taps_in,
    conv,
    conv_in,
    spectra,
    windows,
    product,
    forward_mat,
    inverse_mat,
    send_sem,
    signal_sem,
    taps_sem,
    conv_sem,
    load_sem,
):
    position = lax.axis_index("seq")
    group = lax.axis_index("ch")
    peers = seq_count * group_count
    me = position * group_count + group
    rows = key_ref.shape[0]
    block = rows * group_count
    half = block // 2
    half_seq = seq_count // 2
    upper = position // half_seq
    turns = 2 if group_count % 2 == 0 else 1
    per_turn = group_count // turns

    loads = [
        pltpu.make_async_copy(source, target, load_sem.at[n])
        for n, (source, target) in enumerate(
            [
                (key_hbm, key_ref),
                (value_hbm, value_ref),
                (forward_hbm, forward_mat),
                (inverse_hbm, inverse_mat),
                (query_hbm, query_ref),
                (gain_hbm, gain_ref),
            ]
        )
    ]
    loads[0].start()
    loads[1].start()
    barrier = pltpu.get_barrier_semaphore()

    def greet(step, carry):
        there = lax.rem(position + step // group_count, seq_count)
        across = lax.rem(group + lax.rem(step, group_count), group_count)
        pl.semaphore_signal(barrier, inc=1, device_id=(there, across), device_id_type=MESH)
        return carry

    lax.fori_loop(1, peers, greet, 0)
    pl.semaphore_wait(barrier, peers - 1)

    my_rows = pl.ds(pl.multiple_of(me * rows, rows), rows)
    my_lanes = pl.ds(pl.multiple_of(me * LANES, LANES), LANES)

    def send(with_taps, with_signal, step, carry):
        turn = step // (seq_count * per_turn)
        inner = lax.rem(step, seq_count * per_turn)
        hop = inner // per_turn
        across = turns * lax.rem(group // turns + lax.rem(inner, per_turn), per_turn) + turn
        side = lax.rem(upper + 1 + lax.rem(hop, 2), 2)
        there = side * half_seq + lax.rem(position + hop // 2, half_seq)
        peer = there * group_count + across
        lanes = pl.ds(pl.multiple_of(peer * LANES, LANES), LANES)

        @pl.when(peer != me)
        def _():
            if with_taps:
                pltpu.make_async_remote_copy(
                    src_ref=taps_hbm.at[:, lanes],
                    dst_ref=taps_in.at[my_rows, :],
                    send_sem=send_sem.at[1],
                    recv_sem=taps_sem.at[position],
                    device_id=(there, across),
                    device_id_type=MESH,
                ).start()
            if with_signal:
                pltpu.make_async_remote_copy(
                    src_ref=signal.at[:, lanes],
                    dst_ref=signal_in.at[my_rows, :],
                    send_sem=send_sem.at[0],
                    recv_sem=signal_sem.at[position],
                    device_id=(there, across),
                    device_id_type=MESH,
                ).start()

        return carry

    first = peers // turns
    lax.fori_loop(0, first, functools.partial(send, True, False), 0)
    loads[0].wait()
    loads[1].wait()
    signal[...] = key_ref[...].astype(jnp.float32) * value_ref[...].astype(jnp.float32)
    for load in loads[2:]:
        load.start()
    pltpu.make_async_copy(
        signal.at[:, my_lanes], signal_in.at[my_rows, :], signal_sem.at[position]
    ).start()
    pltpu.make_async_copy(
        taps_hbm.at[:, my_lanes], taps_in.at[my_rows, :], taps_sem.at[position]
    ).start()
    lax.fori_loop(0, first, functools.partial(send, False, True), 0)
    lax.fori_loop(first, peers, functools.partial(send, True, True), 0)
    for load in loads[2:]:
        load.wait()

    def transform(d, carry):
        here = pl.ds(pl.multiple_of(d * block, block), block)
        pltpu.make_async_copy(signal_in.at[here, :], signal_in.at[here, :], signal_sem.at[d]).wait()
        pltpu.make_async_copy(taps_in.at[here, :], taps_in.at[here, :], taps_sem.at[d]).wait()
        both = jnp.concatenate([signal_in[here, :], taps_in[here, :]], axis=1)
        spectrum = jnp.dot(
            forward_mat[...], three_parts(both), preferred_element_type=jnp.float32
        )
        spectra[d] = spectrum[:, :LANES]
        tap_spectrum = spectrum[:, LANES:]
        windows[d] += tap_spectrum
        windows[d + 1, 0:half] = -tap_spectrum[block : block + half]
        windows[d + 1, half:block] = tap_spectrum[block + half :]
        windows[d + 1, block : block + half] = tap_spectrum[0:half]
        windows[d + 1, block + half :] = -tap_spectrum[half:block]
        return carry

    chunk_rows = 64

    def output(d, carry):
        for chunk in range(block // chunk_rows):
            real = pl.ds(chunk * chunk_rows, chunk_rows)
            imag = pl.ds(block + chunk * chunk_rows, chunk_rows)

            def pair(j, totals):
                s_real = spectra[j, real, :]
                s_imag = spectra[j, imag, :]
                f_real = windows[d - j, real, :]
                f_imag = windows[d - j, imag, :]
                return (
                    totals[0] + (s_real * f_real - s_imag * f_imag),
                    totals[1] + (s_real * f_imag + s_imag * f_real),
                )

            zero = jnp.zeros((chunk_rows, LANES), jnp.float32)
            product[real, :], product[imag, :] = lax.fori_loop(0, d + 1, pair, (zero, zero))
        here = pl.ds(pl.multiple_of(d * block, block), block)
        conv[here, :] = jnp.dot(
            inverse_mat[...], three_parts(product[...]), preferred_element_type=jnp.float32
        )
        for c in range(group_count):
            owner = d * group_count + c
            piece = conv.at[pl.ds(pl.multiple_of(owner * rows, rows), rows), :]

            @pl.when(owner != me)
            def _():
                pltpu.make_async_remote_copy(
                    src_ref=piece,
                    dst_ref=conv_in.at[:, my_lanes],
                    send_sem=send_sem.at[2],
                    recv_sem=conv_sem.at[position],
                    device_id=(d, c),
                    device_id_type=MESH,
                ).start()

            @pl.when(owner == me)
            def _():
                pltpu.make_async_copy(piece, conv_in.at[:, my_lanes], conv_sem.at[position]).start()

        return carry

    windows[0] = jnp.zeros((2 * block, LANES), jnp.float32)
    lax.fori_loop(0, half_seq, transform, 0)
    lax.fori_loop(0, half_seq * upper, output, 0)
    lax.fori_loop(half_seq, seq_count, transform, 0)
    lax.fori_loop(half_seq, seq_count, output, 0)
    lax.fori_loop(0, half_seq * (1 - upper), output, 0)

    width = group_count * LANES

    def finish(d, carry):
        lanes = pl.ds(pl.multiple_of(d * width, width), width)
        pltpu.make_async_copy(conv_in.at[:, lanes], conv_in.at[:, lanes], conv_sem.at[d]).wait()
        skipped = gain_ref[0:1, lanes] * signal[:, lanes]
        out_ref[:, lanes] = (
            query_ref[:, lanes].astype(jnp.float32) * (conv_in[:, lanes] + skipped)
        ).astype(jnp.bfloat16)
        return carry

    lax.fori_loop(0, seq_count, finish, 0)

    sent = pl.ds(0, (peers - 1) * rows)
    for which in range(3):
        pltpu.make_async_copy(
            signal_in.at[sent, :], signal_in.at[sent, :], send_sem.at[which]
        ).wait()


def fused_shards(query_rows, key_rows, value_rows, filter_taps, skip_gain):
    seq_count = lax.axis_size("seq")
    group_count = lax.axis_size("ch")
    rows, full_width = key_rows.shape
    block = rows * group_count
    tokens = block * seq_count
    forward, inverse = block_transforms(block)
    in_vmem = pl.BlockSpec(memory_space=pltpu.VMEM)
    in_hbm = pl.BlockSpec(memory_space=pltpu.HBM)
    return pl.pallas_call(
        functools.partial(conv_kernel, seq_count, group_count),
        out_shape=jax.ShapeDtypeStruct((rows, full_width), jnp.bfloat16),
        in_specs=[in_hbm] * 7,
        out_specs=in_vmem,
        scratch_shapes=[
            pltpu.VMEM((rows, full_width), jnp.bfloat16),
            pltpu.VMEM((rows, full_width), jnp.bfloat16),
            pltpu.VMEM((rows, full_width), jnp.bfloat16),
            pltpu.VMEM((1, full_width), jnp.float32),
            pltpu.VMEM((rows, full_width), jnp.float32),
            pltpu.VMEM((tokens, LANES), jnp.float32),
            pltpu.VMEM((tokens, LANES), jnp.float32),
            pltpu.VMEM((tokens, LANES), jnp.float32),
            pltpu.VMEM((rows, full_width), jnp.float32),
            pltpu.VMEM((seq_count, 2 * block, LANES), jnp.float32),
            pltpu.VMEM((seq_count + 1, 2 * block, LANES), jnp.float32),
            pltpu.VMEM((2 * block, LANES), jnp.float32),
            pltpu.VMEM(forward.shape, jnp.bfloat16),
            pltpu.VMEM(inverse.shape, jnp.bfloat16),
            pltpu.SemaphoreType.DMA((3,)),
            pltpu.SemaphoreType.DMA((seq_count,)),
            pltpu.SemaphoreType.DMA((seq_count,)),
            pltpu.SemaphoreType.DMA((seq_count,)),
            pltpu.SemaphoreType.DMA((6,)),
        ],
        compiler_params=pltpu.CompilerParams(
            collective_id=0, has_side_effects=True, vmem_limit_bytes=127 * 512 * 1024
        ),
    )(
        key_rows,
        value_rows,
        filter_taps,
        query_rows,
        skip_gain.reshape(1, full_width),
        jnp.asarray(forward),
        jnp.asarray(inverse),
    )


def solution(mesh):
    device_count = mesh.shape["seq"] * mesh.shape["ch"]
    in_specs = (
        P(("seq", "ch"), None),
        P(("seq", "ch"), None),
        P(("seq", "ch"), None),
        P(("seq", "ch"), None),
        P(),
    )
    out_specs = P(("seq", "ch"), None)

    def program(query_rows, key_rows, value_rows, filter_taps, skip_gain):
        tokens, channels = key_rows.shape
        one_tile_each = channels == LANES * device_count and mesh.shape["seq"] % 2 == 0
        tiled_rows = tokens % (16 * device_count) == 0
        body = fused_shards if one_tile_each and tiled_rows else staged_shards
        return jax.shard_map(
            body, mesh=mesh, in_specs=in_specs, out_specs=out_specs, check_vma=False
        )(query_rows, key_rows, value_rows, filter_taps, skip_gain)

    return program
```
